256 devices in a mesh: pool: 8 (over y, core), group: 32 (over z, x).
Axes of the slice: x: 4, y: 4, z: 8, core: 2. Of those that a mesh axis runs over, the one named last changes fastest.
Arguments:
- queries: bfloat16 [32, 4, 8192], P('group', None, 'pool'), may hold values from -5.6 to 5.6
- new_keys: bfloat16 [32, 4, 1024], P('group', None, 'pool'), may hold values from -6 to 6
- new_values: bfloat16 [32, 4, 1024], P('group', None, 'pool'), may hold values from -8 to 8
- key_cache: bfloat16 [1024, 512, 1024], P('group', None, 'pool'), may hold values from -34 to 34
- value_cache: bfloat16 [1024, 512, 1024], P('group', None, 'pool'), may hold values from -8 to 8
- lengths: int32 [32], replicated, may hold values from 1 to 16384, as said below
- slot_request: int32 [1024], P('group'), may hold values from 0 to 31
- slot_block: int32 [1024], P('group'), may hold values from 0 to 32, as said below
- out_weight: bfloat16 [8192, 8192], P('pool', 'group'), may hold values from -0.0625 to 0.0625
Outputs:
- projected: bfloat16 [128, 8192], P('pool', 'group')
The draws below stay inside these ranges and needn't reach their ends.
Inputs may be any that keep to these rules, and one draw needn't show every extreme that they name: `lengths`: some request has exactly 16384 cached tokens. `slot_block`: block b of a request holds its tokens b * 512 to b * 512 + 511. Each block b with b * 512 < lengths[r] of each request r sits in exactly one slot; every other slot has block number 32 and holds no tokens.
All inputs are finite; a program needn't handle non-finite values.
Results may differ from the reference program's by a relative error of at most 0.0052.
Values may be sent and summed in bfloat16 or wider, within the bound.
A program may use at most 64 MiB of HBM per device.

```python
import math
import jax
import jax.numpy as jnp
from jax import lax

D = 8192
H = 64
KVH = 8
HD = 128
BLK = 512
STEPS = 4
SLOTS = 32
GQA = 8
MAXB = 32
REQS = 32
CSLOTS = 1024
N_GROUP = 32


def placement_lists(key):
    key = jax.random.fold_in(key, 101)
    subkeys = jax.random.split(key, 7)
    request_index = jnp.arange(REQS)
    counts = jax.random.randint(subkeys[0], (REQS,), 1, MAXB + 1)
    longest = jax.random.randint(subkeys[1], (), 0, REQS)
    counts = jnp.where(request_index == longest, MAXB, counts)
    tail_tokens = jax.random.randint(subkeys[2], (REQS,), 1, BLK + 1)
    tail_tokens = jnp.where(request_index == longest, BLK, tail_tokens)
    lengths = ((counts - 1) * BLK + tail_tokens).astype(jnp.int32)
    block_ends = jnp.cumsum(counts)
    block_starts = block_ends - counts
    position = jnp.arange(CSLOTS)
    listed_owner = jnp.sum((position[:, None] >= block_ends[None, :]).astype(jnp.int32), axis=1)
    occupied = listed_owner < REQS
    owner_safe = jnp.minimum(listed_owner, REQS - 1)
    listed_index = position - jnp.take(block_starts, owner_safe)
    filler = jax.random.randint(subkeys[3], (CSLOTS,), 0, REQS)
    listed_request = jnp.where(occupied, owner_safe, filler).astype(jnp.int32)
    listed_block = jnp.where(occupied, listed_index, MAXB).astype(jnp.int32)
    levels = jax.random.randint(subkeys[4], (N_GROUP,), 1, 5)
    busiest = jax.random.randint(subkeys[5], (), 0, N_GROUP)
    levels = jnp.where(jnp.arange(N_GROUP) == busiest, 0, levels)
    jitter = jax.random.randint(subkeys[6], (CSLOTS,), 0, 1024)
    ranking = (jnp.take(levels, position // SLOTS) * 1024 + jitter) * CSLOTS + position
    slot_order = jnp.argsort(ranking)
    slot_request = jnp.zeros((CSLOTS,), jnp.int32).at[slot_order].set(listed_request)
    slot_block = jnp.zeros((CSLOTS,), jnp.int32).at[slot_order].set(listed_block)
    return (lengths, slot_request, slot_block)


def query_values(key):
    key = jax.random.fold_in(key, 202)
    earlier = jax.random.fold_in(key, 0)
    array_shape = (REQS, STEPS, H * HD)
    normal_part = 1.4 * jax.random.truncated_normal(earlier, -4.0, 4.0, array_shape, jnp.float32)
    return normal_part


def draw_lengths(key, part):
    lengths, slot_request, slot_block = placement_lists(key)
    return lengths


def draw_slot_request(key, part):
    lengths, slot_request, slot_block = placement_lists(key)
    return slot_request


def draw_slot_block(key, part):
    lengths, slot_request, slot_block = placement_lists(key)
    return slot_block


def draw_queries(key, part):
    return query_values(key).astype(jnp.bfloat16)


def draw_key_cache(key, part):
    key = jax.random.fold_in(key, 3)
    subkeys = jax.random.split(key, 1)
    array_shape = (CSLOTS, BLK, KVH * HD)
    cache_keys = 1.4 * jax.random.truncated_normal(subkeys[0], -4.0, 4.0, array_shape, jnp.float32)
    return cache_keys.astype(jnp.bfloat16)


def steps_of(key, dims, shards, smallest, largest):
    def one(axis_at, parts):
        draws = jax.random.uniform(jax.random.fold_in(jax.random.fold_in(key, 6), axis_at), (parts,), jnp.float32, smallest / len(shards), largest / len(shards))
        return jnp.repeat(jnp.exp(draws), dims[axis_at] // parts).reshape((-1,) + (1,) * (len(dims) - axis_at - 1))

    level = one(*shards[0])
    for cut in shards[1:]:
        level = level * one(*cut)
    return level


def bell_draw(rng, dims, deviation, bound, cuts=(), dtype=jnp.bfloat16):
    gain = steps_of(rng, dims, cuts, -0.22, 0.18) if cuts else 1.0
    array = jax.random.normal(rng, dims, jnp.float32) * deviation * gain
    return jnp.minimum(jnp.maximum(array, -bound), bound).astype(dtype)


def setup_inputs(seed: int = 0) -> dict:
    key_list = jax.random.split(jax.random.key(seed), 10)
    return {
        "queries": draw_queries(jax.random.fold_in(key_list[9], 71), 0),
        "new_keys": bell_draw(key_list[1], (REQS, STEPS, KVH * HD), 1.4, 6.0, ((0, 32), (2, 8))),
        "new_values": bell_draw(key_list[2], (REQS, STEPS, KVH * HD), 2.0, 8.0, ((0, 32), (2, 8))),
        "key_cache": draw_key_cache(jax.random.fold_in(key_list[9], 71), 0),
        "value_cache": bell_draw(key_list[4], (CSLOTS, BLK, KVH * HD), 2.0, 8.0, ((0, 32), (2, 8))),
        "lengths": draw_lengths(jax.random.fold_in(key_list[9], 71), 0),
        "slot_request": draw_slot_request(jax.random.fold_in(key_list[9], 71), 0),
        "slot_block": draw_slot_block(jax.random.fold_in(key_list[9], 71), 0),
        "out_weight": bell_draw(key_list[8], (H * HD, D), (H * HD) ** -0.5, 0.0625, ((0, 8), (1, 32))),
    }


masked_score = -1e+30

def slot_terms(panel_rows, key_rows, value_rows, live_count):
    slot_count = key_rows.shape[0]
    block_width = key_rows.shape[1]
    kv_heads = key_rows.shape[2] // HD
    query_heads = panel_rows.reshape(slot_count, STEPS, kv_heads, GQA, HD).astype(jnp.float32)
    key_heads = key_rows.reshape(slot_count, block_width, kv_heads, HD).astype(jnp.float32)
    scores = jnp.einsum('sikgd,stkd->sikgt', query_heads, key_heads) * (1.0 / math.sqrt(HD))
    live_mask = (jnp.arange(block_width)[None, :] < live_count[:, None])[:, None, None, None, :]
    scores = jnp.where(live_mask, scores, masked_score)
    slot_top = lax.optimization_barrier(jnp.max(scores, axis=-1))
    weights = jnp.where(live_mask, jnp.exp(scores - slot_top[..., None]), 0.0)
    slot_total = lax.optimization_barrier(jnp.sum(weights, axis=-1))
    rounded = lax.optimization_barrier(weights.astype(jnp.bfloat16)).astype(jnp.float32)
    value_heads = value_rows.reshape(slot_count, block_width, kv_heads, HD).astype(jnp.float32)
    slot_out = jnp.einsum('sikgt,stkd->sikgd', rounded, value_heads)
    return (slot_top, slot_total, slot_out)

def new_terms(query_rows, key_rows, value_rows):
    request_count = query_rows.shape[0]
    kv_heads = key_rows.shape[2] // HD
    query_heads = query_rows.reshape(request_count, STEPS, kv_heads, GQA, HD).astype(jnp.float32)
    key_heads = key_rows.reshape(request_count, STEPS, kv_heads, HD).astype(jnp.float32)
    scores = jnp.einsum('rikgd,rjkd->rikgj', query_heads, key_heads) * (1.0 / math.sqrt(HD))
    causal = (jnp.arange(STEPS)[:, None] >= jnp.arange(STEPS)[None, :])[None, :, None, None, :]
    scores = jnp.where(causal, scores, masked_score)
    new_top = lax.optimization_barrier(jnp.max(scores, axis=-1))
    weights = jnp.where(causal, jnp.exp(scores - new_top[..., None]), 0.0)
    new_total = lax.optimization_barrier(jnp.sum(weights, axis=-1))
    rounded = lax.optimization_barrier(weights.astype(jnp.bfloat16)).astype(jnp.float32)
    value_heads = value_rows.reshape(request_count, STEPS, kv_heads, HD).astype(jnp.float32)
    new_out = jnp.einsum('rikgj,rjkd->rikgd', rounded, value_heads)
    return (new_top, new_total, new_out)

def reference(queries, new_keys, new_values, key_cache, value_cache, lengths, slot_request, slot_block, out_weight):
    live_count = jnp.clip(jnp.take(lengths, slot_request) - slot_block * BLK, 0, BLK).astype(jnp.int32)

    def per_holder(pieces):
        key_rows, value_rows, requests, counts = pieces
        panel_rows = jnp.take(queries, requests, axis=0)
        return slot_terms(panel_rows, key_rows, value_rows, counts)
    tops, totals, outs = lax.map(per_holder, (key_cache.reshape(N_GROUP, SLOTS, BLK, KVH * HD), value_cache.reshape(N_GROUP, SLOTS, BLK, KVH * HD), slot_request.reshape(N_GROUP, SLOTS), live_count.reshape(N_GROUP, SLOTS)))
    tops = tops.reshape((CSLOTS,) + tops.shape[2:])
    totals = totals.reshape((CSLOTS,) + totals.shape[2:])
    outs = outs.reshape((CSLOTS,) + outs.shape[2:])
    new_top, new_total, new_out = new_terms(queries, new_keys, new_values)
    matches = (slot_request[:, None] == jnp.arange(REQS)[None, :])[:, :, None, None, None]
    best = jnp.maximum(new_top, lax.optimization_barrier(jnp.max(jnp.where(matches, tops[:, None], masked_score), axis=0)))
    slot_scale = jnp.exp(tops - jnp.take(best, slot_request, axis=0))
    new_scale = jnp.exp(new_top - best)
    denominator = new_scale * new_total + jax.ops.segment_sum(slot_scale * totals, slot_request, num_segments=REQS)
    numerator = new_scale[..., None] * new_out + jax.ops.segment_sum(slot_scale[..., None] * outs, slot_request, num_segments=REQS)
    attention = (numerator / denominator[..., None]).astype(jnp.bfloat16).reshape(REQS * STEPS, H * HD)
    return jnp.dot(attention, out_weight, preferred_element_type=jnp.float32).astype(jnp.bfloat16)
```

```python
import functools
import math

import jax
import jax.numpy as jnp
from jax import lax
from jax.experimental import pallas as pl
from jax.experimental.pallas import tpu as pltpu
from jax.sharding import PartitionSpec as P

HD = 128
STEPS = 4
GQA = 8
ROWS = STEPS * GQA
NX = 4
NZ = 8

MESH = pl.DeviceIdType.MESH
masked_score = -1e30
floor_score = -1e29
log2e = math.log2(math.e)


def wait_bytes(ref, sem):
    pltpu.make_async_copy(ref, ref, sem).wait()


def kernel(
    q_ref,
    nk_ref,
    nv_ref,
    len_ref,
    sreq_ref,
    sblk_ref,
    k_hbm,
    v_hbm,
    w_hbm,
    o_ref,
    k_vm,
    v_vm,
    w_vm,
    q_f32,
    q_all,
    scores,
    tops,
    outs,
    table_f32,
    table,
    stats,
    got,
    got_stats,
    att_all,
    att_f32,
    y_f32,
    y_got,
    load_sem,
    send_sem,
    recv_sem,
):
    slots, block_width = k_vm.shape[0], k_vm.shape[1]
    requests = q_all.shape[0]
    pools = y_got.shape[0]
    g = lax.axis_index("group")
    p = lax.axis_index("pool")
    z, x = g // NX, g % NX
    scale = log2e / math.sqrt(HD)

    loads = [
        pltpu.make_async_copy(k_hbm, k_vm, load_sem.at[0]),
        pltpu.make_async_copy(v_hbm, v_vm, load_sem.at[1]),
        pltpu.make_async_copy(w_hbm, w_vm, load_sem.at[2]),
    ]
    for load in loads:
        load.start()

    offsets = [(dz, dx) for dz in (4, 3, 5, 2, 6, 1, 7, 0) for dx in (2, 1, 3, 0)]
    peers = [
        lax.rem(z + dz, NZ) * NX + lax.rem(x + dx, NX) for dz, dx in offsets if (dz, dx) != (0, 0)
    ]
    pool_peers = [lax.rem(p + d, pools) for d in (4, 5, 3, 2, 6, 7, 1)]

    barrier = pltpu.get_barrier_semaphore()
    for peer in peers:
        pl.semaphore_signal(barrier, inc=1, device_id={"group": peer}, device_id_type=MESH)
    for peer in pool_peers:
        pl.semaphore_signal(barrier, inc=1, device_id={"pool": peer}, device_id_type=MESH)

    q_rows = q_ref[0].astype(jnp.float32)
    for h in range(GQA):
        q_f32[pl.ds(h, STEPS, stride=GQA), :] = q_rows[:, h * HD : (h + 1) * HD]
    own_q = q_f32[...]
    q_all[g] = own_q.astype(jnp.bfloat16)

    pl.semaphore_wait(barrier, len(peers) + len(pool_peers))

    def to_group(src, dst, phase):
        for peer in peers:
            pltpu.make_async_remote_copy(
                src_ref=src(peer),
                dst_ref=dst,
                send_sem=send_sem.at[phase],
                recv_sem=recv_sem.at[phase],
                device_id={"group": peer},
                device_id_type=MESH,
            ).start()

    to_group(lambda peer: q_all.at[g], q_all.at[g], 0)

    row_step = lax.broadcasted_iota(jnp.int32, (ROWS, 1), 0) // GQA
    nk = nk_ref[0].astype(jnp.float32)
    nv = nv_ref[0].astype(jnp.float32)
    new_scores = []
    for j in range(STEPS):
        s = jnp.sum(own_q * nk[j : j + 1, :], axis=1, keepdims=True) * scale
        new_scores.append(jnp.where(row_step >= j, s, masked_score))
    new_top = functools.reduce(jnp.maximum, new_scores)
    new_total = jnp.zeros((ROWS, 1), jnp.float32)
    new_out = jnp.zeros((ROWS, HD), jnp.float32)
    for j in range(STEPS):
        w = jnp.exp2(new_scores[j] - new_top)
        new_total += w
        new_out += w.astype(jnp.bfloat16).astype(jnp.float32) * nv[j : j + 1, :]

    lane = lax.broadcasted_iota(jnp.int32, (ROWS, HD), 1)
    token = lax.broadcasted_iota(jnp.int32, (ROWS, block_width), 1)
    owner = jnp.full((ROWS, HD), -1, jnp.int32)
    for s in range(slots):
        owner = jnp.where(lane == s, sreq_ref[s], owner)

    loads[0].wait()
    others = pl.ds(0, len(peers))
    wait_bytes(q_all.at[others], recv_sem.at[0])

    unroll = 4

    def score_slots(it, top):
        for u in range(unroll):
            s = it * unroll + u
            r = sreq_ref[s]
            live = jnp.clip(len_ref[r] - sblk_ref[s] * block_width, 0, block_width)
            sc = lax.dot_general(
                q_all[r], k_vm[s], (((1,), (1,)), ((), ())), preferred_element_type=jnp.float32
            )
            sc = jnp.where(token < live, sc * scale, masked_score)
            scores[s] = sc
            top = jnp.where(lane == s, jnp.max(sc, axis=1, keepdims=True), top)
        return top

    top = lax.fori_loop(
        0, slots // unroll, score_slots, jnp.full((ROWS, HD), masked_score, jnp.float32)
    )

    request_top = jnp.full((ROWS, HD), masked_score, jnp.float32)
    for r in range(requests):
        m = jnp.max(jnp.where(owner == r, top, masked_score), axis=1, keepdims=True)
        request_top = jnp.where(lane == r, m, request_top)
        tops[r] = jnp.broadcast_to(jnp.maximum(m, floor_score), (ROWS, HD))

    loads[1].wait()

    def weigh_slots(it, total):
        for u in range(unroll):
            s = it * unroll + u
            m = tops[sreq_ref[s]]
            w = jnp.exp2(scores[s] - jnp.concatenate([m] * (block_width // HD), axis=1))
            total = jnp.where(lane == s, jnp.sum(w, axis=1, keepdims=True), total)
            out = jnp.dot(w.astype(jnp.bfloat16), v_vm[s], preferred_element_type=jnp.float32)
            outs[pl.ds(pl.multiple_of(s * ROWS, ROWS), ROWS), :] = out
        return total

    total = lax.fori_loop(
        0, slots // unroll, weigh_slots, jnp.zeros((ROWS, HD), jnp.float32)
    )

    hot = (lax.broadcasted_iota(jnp.int32, (ROWS, HD), 0) == owner).astype(jnp.float32)
    request_total = lax.dot_general(
        total,
        hot,
        (((1,), (1,)), ((), ())),
        precision=lax.Precision.HIGHEST,
        preferred_element_type=jnp.float32,
    )
    request_total = jnp.concatenate(
        [request_total, jnp.zeros((ROWS, HD - requests), jnp.float32)], axis=1
    )
    pair = jnp.concatenate(
        [request_top, request_total, jnp.zeros((HD - 2 * ROWS, HD), jnp.float32)], axis=0
    )
    stats[...] = pair.T[:requests].reshape(requests, 1, HD)
    hot_slots = hot[:, :slots].astype(jnp.bfloat16)
    hot_twice = jnp.concatenate([hot_slots, hot_slots], axis=1)
    for j in range(ROWS):
        o = outs[pl.ds(j, slots, stride=ROWS), :]
        high = o.astype(jnp.bfloat16)
        low = (o - high.astype(jnp.float32)).astype(jnp.bfloat16)
        table_f32[pl.ds(j, requests, stride=ROWS), :] = jnp.dot(
            hot_twice, jnp.concatenate([high, low], axis=0), preferred_element_type=jnp.float32
        )
    table[...] = table_f32[...].astype(jnp.bfloat16).reshape(requests, ROWS, HD)

    to_group(lambda peer: stats.at[peer], got_stats.at[g], 1)
    to_group(lambda peer: table.at[peer], got.at[g], 2)
    got[g] = table[g]
    got_stats[g] = stats[g]
    wait_bytes(got_stats.at[others], recv_sem.at[1])

    stat_rows = got_stats[...].reshape(requests, HD)
    turned = jnp.concatenate([stat_rows, jnp.zeros((HD - requests, HD), jnp.float32)], axis=0).T
    held_top = jnp.where(lane < requests, turned[:ROWS], masked_score)
    held_total = turned[ROWS : 2 * ROWS]
    best = jnp.maximum(jnp.max(held_top, axis=1, keepdims=True), new_top)
    held_scale = jnp.exp2(held_top - best)
    new_scale = jnp.exp2(new_top - best)
    denominator = new_scale * new_total + jnp.sum(held_scale * held_total, axis=1, keepdims=True)
    inverse = 1.0 / denominator
    wait_bytes(got.at[others], recv_sem.at[2])
    numerator = new_scale * new_out
    for h in range(requests):
        numerator += held_scale[:, h : h + 1] * got[h].astype(jnp.float32)
    att_all[g] = (numerator * inverse).astype(jnp.bfloat16)

    to_group(lambda peer: att_all.at[g], att_all.at[g], 3)
    loads[2].wait()
    wait_bytes(att_all.at[others], recv_sem.at[3])

    att_f32[...] = att_all[...].reshape(requests * ROWS, HD).astype(jnp.float32)
    att = jnp.concatenate(
        [
            att_f32[pl.ds(h, requests * STEPS, stride=GQA), :].astype(jnp.bfloat16)
            for h in range(GQA)
        ],
        axis=1,
    )
    y = jnp.dot(att, w_vm[...], preferred_element_type=jnp.float32)
    y_f32[...] = y.reshape(y_f32.shape)

    for peer in pool_peers:
        pltpu.make_async_remote_copy(
            src_ref=y_f32.at[peer],
            dst_ref=y_got.at[p],
            send_sem=send_sem.at[4],
            recv_sem=recv_sem.at[4],
            device_id={"pool": peer},
            device_id_type=MESH,
        ).start()
    wait_bytes(y_got.at[pl.ds(0, pools - 1)], recv_sem.at[4])
    result = y_f32[p]
    for peer in pool_peers:
        result += y_got[peer]
    o_ref[...] = result.astype(o_ref.dtype)

    wait_bytes(q_all.at[others], send_sem.at[0])
    wait_bytes(got_stats.at[others], send_sem.at[1])
    wait_bytes(got.at[others], send_sem.at[2])
    wait_bytes(att_all.at[others], send_sem.at[3])
    wait_bytes(y_got.at[pl.ds(0, pools - 1)], send_sem.at[4])


def body(
    queries,
    new_keys,
    new_values,
    key_cache,
    value_cache,
    lengths,
    slot_request,
    slot_block,
    out_weight,
):
    slots, block_width, _ = key_cache.shape
    requests = lengths.shape[0]
    columns = out_weight.shape[1]
    pools = lax.axis_size("pool")
    out_rows = requests * STEPS // pools
    vmem = pl.BlockSpec(memory_space=pltpu.VMEM)
    smem = pl.BlockSpec(memory_space=pltpu.SMEM)
    hbm = pl.BlockSpec(memory_space=pl.ANY)
    return pl.pallas_call(
        kernel,
        out_shape=jax.ShapeDtypeStruct((out_rows, columns), jnp.bfloat16),
        in_specs=[vmem, vmem, vmem, smem, smem, smem, hbm, hbm, hbm],
        out_specs=vmem,
        scratch_shapes=[
            pltpu.VMEM(key_cache.shape, jnp.bfloat16),
            pltpu.VMEM(value_cache.shape, jnp.bfloat16),
            pltpu.VMEM(out_weight.shape, jnp.bfloat16),
            pltpu.VMEM((ROWS, HD), jnp.float32),
            pltpu.VMEM((requests, ROWS, HD), jnp.bfloat16),
            pltpu.VMEM((slots, ROWS, block_width), jnp.float32),
            pltpu.VMEM((requests, ROWS, HD), jnp.float32),
            pltpu.VMEM((slots * ROWS, HD), jnp.float32),
            pltpu.VMEM((requests * ROWS, HD), jnp.float32),
            pltpu.VMEM((requests, ROWS, HD), jnp.bfloat16),
            pltpu.VMEM((requests, 1, HD), jnp.float32),
            pltpu.VMEM((requests, ROWS, HD), jnp.bfloat16),
            pltpu.VMEM((requests, 1, HD), jnp.float32),
            pltpu.VMEM((requests, ROWS, HD), jnp.bfloat16),
            pltpu.VMEM((requests * ROWS, HD), jnp.float32),
            pltpu.VMEM((pools, out_rows, columns), jnp.float32),
            pltpu.VMEM((pools, out_rows, columns), jnp.float32),
            pltpu.SemaphoreType.DMA((3,)),
            pltpu.SemaphoreType.DMA((5,)),
            pltpu.SemaphoreType.DMA((5,)),
        ],
        compiler_params=pltpu.CompilerParams(
            collective_id=0, has_side_effects=True, vmem_limit_bytes=48 << 20
        ),
        name="paged_attention",
    )(
        queries,
        new_keys,
        new_values,
        lengths,
        slot_request,
        slot_block,
        key_cache,
        value_cache,
        out_weight,
    )


def solution(mesh):
    in_specs = (
        P("group", None, "pool"),
        P("group", None, "pool"),
        P("group", None, "pool"),
        P("group", None, "pool"),
        P("group", None, "pool"),
        P(),
        P("group"),
        P("group"),
        P("pool", "group"),
    )
    out_specs = P("pool", "group")
    return jax.shard_map(body, mesh=mesh, in_specs=in_specs, out_specs=out_specs, check_vma=False)
```

```python
import functools
import math

import jax
import jax.numpy as jnp
from jax import lax
from jax.experimental import pallas as pl
from jax.experimental.pallas import tpu as pltpu
from jax.sharding import PartitionSpec as P

HD = 128
STEPS = 4
GQA = 8
ROWS = STEPS * GQA
NX = 4
NZ = 8

MESH = pl.DeviceIdType.MESH
masked_score = -1e30
floor_score = -1e29
log2e = math.log2(math.e)


def wait_bytes(ref, sem):
    pltpu.make_async_copy(ref, ref, sem).wait()


def kernel(
    q_hbm,
    nk_hbm,
    nv_hbm,
    len_hbm,
    sreq_hbm,
    sblk_hbm,
    k_hbm,
    v_hbm,
    w_hbm,
    o_ref,
    k_vm,
    v_vm,
    w_vm,
    q_f32,
    q_all,
    scores,
    tops,
    outs,
    table_f32,
    table,
    stats,
    got,
    got_stats,
    att_all,
    att_f32,
    y_f32,
    y_got,
    q_in,
    nk_in,
    nv_in,
    len_in,
    sreq_in,
    sblk_in,
    load_sem,
    send_sem,
    recv_sem,
):
    slots, block_width = k_vm.shape[0], k_vm.shape[1]
    requests = q_all.shape[0]
    pools = y_got.shape[0]
    g = lax.axis_index("group")
    p = lax.axis_index("pool")
    z, x = g // NX, g % NX
    scale = log2e / math.sqrt(HD)

    loads = [
        pltpu.make_async_copy(k_hbm, k_vm, load_sem.at[0]),
        pltpu.make_async_copy(v_hbm, v_vm, load_sem.at[1]),
        pltpu.make_async_copy(w_hbm, w_vm, load_sem.at[2]),
        pltpu.make_async_copy(q_hbm, q_in, load_sem.at[3]),
        pltpu.make_async_copy(nk_hbm, nk_in, load_sem.at[4]),
        pltpu.make_async_copy(nv_hbm, nv_in, load_sem.at[5]),
        pltpu.make_async_copy(len_hbm, len_in, load_sem.at[6]),
        pltpu.make_async_copy(sreq_hbm, sreq_in, load_sem.at[7]),
        pltpu.make_async_copy(sblk_hbm, sblk_in, load_sem.at[8]),
    ]
    for load in loads[3:] + loads[:3]:
        load.start()

    offsets = [(dz, dx) for dz in (4, 3, 5, 2, 6, 1, 7, 0) for dx in (2, 1, 3, 0)]
    peers = [
        lax.rem(z + dz, NZ) * NX + lax.rem(x + dx, NX) for dz, dx in offsets if (dz, dx) != (0, 0)
    ]
    pool_peers = [lax.rem(p + d, pools) for d in (4, 5, 3, 2, 6, 7, 1)]

    barrier = pltpu.get_barrier_semaphore()
    for peer in peers:
        pl.semaphore_signal(barrier, inc=1, device_id={"group": peer}, device_id_type=MESH)
    for peer in pool_peers:
        pl.semaphore_signal(barrier, inc=1, device_id={"pool": peer}, device_id_type=MESH)

    loads[3].wait()
    q_rows = q_in[0].astype(jnp.float32)
    for h in range(GQA):
        q_f32[pl.ds(h, STEPS, stride=GQA), :] = q_rows[:, h * HD : (h + 1) * HD]
    own_q = q_f32[...]
    q_all[g] = own_q.astype(jnp.bfloat16)

    pl.semaphore_wait(barrier, len(peers) + len(pool_peers))

    def to_group(src, dst, phase):
        for peer in peers:
            pltpu.make_async_remote_copy(
                src_ref=src(peer),
                dst_ref=dst,
                send_sem=send_sem.at[phase],
                recv_sem=recv_sem.at[phase],
                device_id={"group": peer},
                device_id_type=MESH,
            ).start()

    to_group(lambda peer: q_all.at[g], q_all.at[g], 0)

    row_step = lax.broadcasted_iota(jnp.int32, (ROWS, 1), 0) // GQA
    for load in loads[4:]:
        load.wait()
    nk = nk_in[0].astype(jnp.float32)
    nv = nv_in[0].astype(jnp.float32)
    new_scores = []
    for j in range(STEPS):
        s = jnp.sum(own_q * nk[j : j + 1, :], axis=1, keepdims=True) * scale
        new_scores.append(jnp.where(row_step >= j, s, masked_score))
    new_top = functools.reduce(jnp.maximum, new_scores)
    new_total = jnp.zeros((ROWS, 1), jnp.float32)
    new_out = jnp.zeros((ROWS, HD), jnp.float32)
    for j in range(STEPS):
        w = jnp.exp2(new_scores[j] - new_top)
        new_total += w
        new_out += w.astype(jnp.bfloat16).astype(jnp.float32) * nv[j : j + 1, :]

    lane = lax.broadcasted_iota(jnp.int32, (ROWS, HD), 1)
    token = lax.broadcasted_iota(jnp.int32, (ROWS, block_width), 1)
    owner = jnp.full((ROWS, HD), -1, jnp.int32)
    for s in range(slots):
        owner = jnp.where(lane == s, sreq_in[s], owner)

    loads[0].wait()
    others = pl.ds(0, len(peers))
    wait_bytes(q_all.at[others], recv_sem.at[0])

    unroll = 16

    def score_slots(it, top):
        for u in range(unroll):
            s = it * unroll + u
            r = sreq_in[s]
            live = jnp.clip(len_in[r] - sblk_in[s] * block_width, 0, block_width)
            sc = lax.dot_general(
                q_all[r], k_vm[s], (((1,), (1,)), ((), ())), preferred_element_type=jnp.float32
            )
            sc = jnp.where(token < live, sc * scale, masked_score)
            scores[s] = sc
            top = jnp.where(lane == s, jnp.max(sc, axis=1, keepdims=True), top)
        return top

    top = lax.fori_loop(
        0, slots // unroll, score_slots, jnp.full((ROWS, HD), masked_score, jnp.float32)
    )

    request_top = jnp.full((ROWS, HD), masked_score, jnp.float32)
    for r in range(requests):
        m = jnp.max(jnp.where(owner == r, top, masked_score), axis=1, keepdims=True)
        request_top = jnp.where(lane == r, m, request_top)
        tops[r] = jnp.broadcast_to(jnp.maximum(m, floor_score), (ROWS, HD))

    loads[1].wait()

    def weigh_slots(it, total):
        for u in range(unroll):
            s = it * unroll + u
            m = tops[sreq_in[s]]
            w = jnp.exp2(scores[s] - jnp.concatenate([m] * (block_width // HD), axis=1))
            total = jnp.where(lane == s, jnp.sum(w, axis=1, keepdims=True), total)
            out = jnp.dot(w.astype(jnp.bfloat16), v_vm[s], preferred_element_type=jnp.float32)
            outs[pl.ds(pl.multiple_of(s * ROWS, ROWS), ROWS), :] = out
        return total

    total = lax.fori_loop(
        0, slots // unroll, weigh_slots, jnp.zeros((ROWS, HD), jnp.float32)
    )

    hot = (lax.broadcasted_iota(jnp.int32, (ROWS, HD), 0) == owner).astype(jnp.float32)
    request_total = lax.dot_general(
        total,
        hot,
        (((1,), (1,)), ((), ())),
        precision=lax.Precision.HIGHEST,
        preferred_element_type=jnp.float32,
    )
    request_total = jnp.concatenate(
        [request_total, jnp.zeros((ROWS, HD - requests), jnp.float32)], axis=1
    )
    pair = jnp.concatenate(
        [request_top, request_total, jnp.zeros((HD - 2 * ROWS, HD), jnp.float32)], axis=0
    )
    stats[...] = pair.T[:requests].reshape(requests, 1, HD)
    hot_slots = hot[:, :slots].astype(jnp.bfloat16)
    hot_twice = jnp.concatenate([hot_slots, hot_slots], axis=1)
    for j in range(ROWS):
        o = outs[pl.ds(j, slots, stride=ROWS), :]
        high = o.astype(jnp.bfloat16)
        low = (o - high.astype(jnp.float32)).astype(jnp.bfloat16)
        table_f32[pl.ds(j, requests, stride=ROWS), :] = jnp.dot(
            hot_twice, jnp.concatenate([high, low], axis=0), preferred_element_type=jnp.float32
        )
    table[...] = table_f32[...].astype(jnp.bfloat16).reshape(requests, ROWS, HD)

    to_group(lambda peer: stats.at[peer], got_stats.at[g], 1)
    to_group(lambda peer: table.at[peer], got.at[g], 2)
    got[g] = table[g]
    got_stats[g] = stats[g]
    wait_bytes(got_stats.at[others], recv_sem.at[1])

    stat_rows = got_stats[...].reshape(requests, HD)
    turned = jnp.concatenate([stat_rows, jnp.zeros((HD - requests, HD), jnp.float32)], axis=0).T
    held_top = jnp.where(lane < requests, turned[:ROWS], masked_score)
    held_total = turned[ROWS : 2 * ROWS]
    best = jnp.maximum(jnp.max(held_top, axis=1, keepdims=True), new_top)
    held_scale = jnp.exp2(held_top - best)
    new_scale = jnp.exp2(new_top - best)
    denominator = new_scale * new_total + jnp.sum(held_scale * held_total, axis=1, keepdims=True)
    inverse = 1.0 / denominator
    wait_bytes(got.at[others], recv_sem.at[2])
    numerator = new_scale * new_out
    for h in range(requests):
        numerator += held_scale[:, h : h + 1] * got[h].astype(jnp.float32)
    att_all[g] = (numerator * inverse).astype(jnp.bfloat16)

    to_group(lambda peer: att_all.at[g], att_all.at[g], 3)
    loads[2].wait()
    wait_bytes(att_all.at[others], recv_sem.at[3])

    att_f32[...] = att_all[...].reshape(requests * ROWS, HD).astype(jnp.float32)
    att = jnp.concatenate(
        [
            att_f32[pl.ds(h, requests * STEPS, stride=GQA), :].astype(jnp.bfloat16)
            for h in range(GQA)
        ],
        axis=1,
    )
    y = jnp.dot(att, w_vm[...], preferred_element_type=jnp.float32)
    y_f32[...] = y.reshape(y_f32.shape)

    for peer in pool_peers:
        pltpu.make_async_remote_copy(
            src_ref=y_f32.at[peer],
            dst_ref=y_got.at[p],
            send_sem=send_sem.at[4],
            recv_sem=recv_sem.at[4],
            device_id={"pool": peer},
            device_id_type=MESH,
        ).start()
    wait_bytes(y_got.at[pl.ds(0, pools - 1)], recv_sem.at[4])
    result = y_f32[p]
    for peer in pool_peers:
        result += y_got[peer]
    o_ref[...] = result.astype(o_ref.dtype)

    wait_bytes(q_all.at[others], send_sem.at[0])
    wait_bytes(got_stats.at[others], send_sem.at[1])
    wait_bytes(got.at[others], send_sem.at[2])
    wait_bytes(att_all.at[others], send_sem.at[3])
    wait_bytes(y_got.at[pl.ds(0, pools - 1)], send_sem.at[4])


def body(
    queries,
    new_keys,
    new_values,
    key_cache,
    value_cache,
    lengths,
    slot_request,
    slot_block,
    out_weight,
):
    slots, block_width, _ = key_cache.shape
    requests = lengths.shape[0]
    columns = out_weight.shape[1]
    pools = lax.axis_size("pool")
    out_rows = requests * STEPS // pools
    vmem = pl.BlockSpec(memory_space=pltpu.VMEM)
    hbm = pl.BlockSpec(memory_space=pltpu.HBM)
    pin = lambda a: pltpu.with_memory_space_constraint(a, pltpu.HBM)
    return pl.pallas_call(
        kernel,
        out_shape=jax.ShapeDtypeStruct((out_rows, columns), jnp.bfloat16),
        in_specs=[hbm] * 9,
        out_specs=vmem,
        scratch_shapes=[
            pltpu.VMEM(key_cache.shape, jnp.bfloat16),
            pltpu.VMEM(value_cache.shape, jnp.bfloat16),
            pltpu.VMEM(out_weight.shape, jnp.bfloat16),
            pltpu.VMEM((ROWS, HD), jnp.float32),
            pltpu.VMEM((requests, ROWS, HD), jnp.bfloat16),
            pltpu.VMEM((slots, ROWS, block_width), jnp.float32),
            pltpu.VMEM((requests, ROWS, HD), jnp.float32),
            pltpu.VMEM((slots * ROWS, HD), jnp.float32),
            pltpu.VMEM((requests * ROWS, HD), jnp.float32),
            pltpu.VMEM((requests, ROWS, HD), jnp.bfloat16),
            pltpu.VMEM((requests, 1, HD), jnp.float32),
            pltpu.VMEM((requests, ROWS, HD), jnp.bfloat16),
            pltpu.VMEM((requests, 1, HD), jnp.float32),
            pltpu.VMEM((requests, ROWS, HD), jnp.bfloat16),
            pltpu.VMEM((requests * ROWS, HD), jnp.float32),
            pltpu.VMEM((pools, out_rows, columns), jnp.float32),
            pltpu.VMEM((pools, out_rows, columns), jnp.float32),
            pltpu.VMEM(queries.shape, jnp.bfloat16),
            pltpu.VMEM(new_keys.shape, jnp.bfloat16),
            pltpu.VMEM(new_values.shape, jnp.bfloat16),
            pltpu.SMEM(lengths.shape, jnp.int32),
            pltpu.SMEM(slot_request.shape, jnp.int32),
            pltpu.SMEM(slot_block.shape, jnp.int32),
            pltpu.SemaphoreType.DMA((9,)),
            pltpu.SemaphoreType.DMA((5,)),
            pltpu.SemaphoreType.DMA((5,)),
        ],
        compiler_params=pltpu.CompilerParams(
            collective_id=0, has_side_effects=True, vmem_limit_bytes=48 << 20
        ),
        name="paged_attention",
    )(
        pin(queries),
        pin(new_keys),
        pin(new_values),
        pin(lengths),
        pin(slot_request),
        pin(slot_block),
        pin(key_cache),
        pin(value_cache),
        pin(out_weight),
    )


def solution(mesh):
    in_specs = (
        P("group", None, "pool"),
        P("group", None, "pool"),
        P("group", None, "pool"),
        P("group", None, "pool"),
        P("group", None, "pool"),
        P(),
        P("group"),
        P("group"),
        P("pool", "group"),
    )
    out_specs = P("pool", "group")
    return jax.shard_map(body, mesh=mesh, in_specs=in_specs, out_specs=out_specs, check_vma=False)
```

```python
import functools
import math

import jax
import jax.numpy as jnp
from jax import lax
from jax.experimental import pallas as pl
from jax.experimental.pallas import tpu as pltpu
from jax.sharding import PartitionSpec as P

HD = 128
STEPS = 4
GQA = 8
HALVES = 2
HEADS = GQA // HALVES
ROWS = STEPS * HEADS
BOTH = HALVES * ROWS
UNROLL = 32
TURNS = 4
NX = 4
NZ = 8

EVERY = [(dz, dx) for dz in (4, 3, 5, 2, 6, 1, 7, 0) for dx in (2, 1, 3, 0) if (dz, dx) != (0, 0)]
LINE_Z = (4, 3, 5, 2, 6, 1, 7)
LINE_X = (2, 1, 3)

MESH = pl.DeviceIdType.MESH
masked_score = -1e30
floor_score = -1e29
log2e = math.log2(math.e)


def wait_bytes(ref, sem):
    pltpu.make_async_copy(ref, ref, sem).wait()


def kernel(
    q_hbm,
    nk_hbm,
    nv_hbm,
    len_hbm,
    sreq_hbm,
    sblk_hbm,
    k_hbm,
    v_hbm,
    w_hbm,
    o_ref,
    k_vm,
    k_turned,
    v_vm,
    w_vm,
    q_f32,
    q_all,
    scores,
    tops,
    outs,
    table_f32,
    table,
    stats,
    got,
    got_stats,
    att_all,
    att_f32,
    y_f32,
    y_got,
    q_in,
    nk_in,
    nv_in,
    len_in,
    sreq_in,
    sblk_in,
    load_sem,
    send_sem,
    recv_sem,
    pool_sem,
    line_sem,
    query_sem,
):
    slots, block_width = k_vm.shape[0], k_vm.shape[1]
    requests = q_all.shape[0]
    pools = y_got.shape[0]
    g = lax.axis_index("group")
    p = lax.axis_index("pool")
    z, x = g // NX, g % NX
    scale = log2e / math.sqrt(HD)

    loads = [
        pltpu.make_async_copy(k_hbm, k_vm, load_sem.at[0]),
        pltpu.make_async_copy(v_hbm, v_vm, load_sem.at[1]),
        pltpu.make_async_copy(w_hbm, w_vm, load_sem.at[2]),
        pltpu.make_async_copy(q_hbm, q_in, load_sem.at[3]),
        pltpu.make_async_copy(nk_hbm, nk_in, load_sem.at[4]),
        pltpu.make_async_copy(nv_hbm, nv_in, load_sem.at[5]),
        pltpu.make_async_copy(len_hbm, len_in, load_sem.at[6]),
        pltpu.make_async_copy(sreq_hbm, sreq_in, load_sem.at[7]),
        pltpu.make_async_copy(sblk_hbm, sblk_in, load_sem.at[8]),
    ]
    for load in loads[3:] + loads[:3]:
        load.start()

    def peer_at(dz, dx):
        return lax.rem(z + dz, NZ) * NX + lax.rem(x + dx, NX)

    peers = [peer_at(dz, dx) for dz, dx in EVERY]
    others = pl.ds(0, len(peers))
    pool_peers = [lax.rem(p + d, pools) for d in (4, 5, 3, 2, 6, 7, 1)]

    barrier = pltpu.get_barrier_semaphore()
    for peer in [peer_at(dz, 0) for dz in LINE_Z] + [peer_at(0, dx) for dx in LINE_X]:
        pl.semaphore_signal(barrier, inc=1, device_id={"group": peer}, device_id_type=MESH)
    for peer in pool_peers:
        pl.semaphore_signal(barrier, inc=1, device_id={"pool": peer}, device_id_type=MESH)

    loads[3].wait()
    q_rows = q_in[0].astype(jnp.float32)
    for half in range(HALVES):
        for h in range(HEADS):
            at = (half * HEADS + h) * HD
            q_f32[pl.ds(half * ROWS + h, STEPS, stride=HEADS), :] = q_rows[:, at : at + HD]
    own_q = q_f32[...]
    q_all[g] = own_q.astype(jnp.bfloat16)

    pl.semaphore_wait(barrier, len(LINE_Z) + len(LINE_X) + len(pool_peers))

    def to_group(src, dst, phase, half):
        for peer in peers:
            pltpu.make_async_remote_copy(
                src_ref=src(peer),
                dst_ref=dst,
                send_sem=send_sem.at[phase, half],
                recv_sem=recv_sem.at[phase, half],
                device_id={"group": peer},
                device_id_type=MESH,
            ).start()

    def send_query(owner, target, sem):
        pltpu.make_async_remote_copy(
            src_ref=q_all.at[owner],
            dst_ref=q_all.at[owner],
            send_sem=query_sem.at[0],
            recv_sem=sem,
            device_id={"group": target},
            device_id_type=MESH,
        ).start()

    for dz in LINE_Z:
        send_query(g, peer_at(dz, 0), line_sem.at[dz])
    for dx in LINE_X:
        send_query(g, peer_at(0, dx), query_sem.at[1])

    for load in loads[4:]:
        load.wait()
    row_step = lax.broadcasted_iota(jnp.int32, (BOTH, 1), 0) % ROWS // HEADS
    nk = nk_in[0].astype(jnp.float32)
    nv = nv_in[0].astype(jnp.float32)
    new_scores = []
    for j in range(STEPS):
        s = jnp.sum(own_q * nk[j : j + 1, :], axis=1, keepdims=True) * scale
        new_scores.append(jnp.where(row_step >= j, s, masked_score))
    new_top = functools.reduce(jnp.maximum, new_scores)
    new_total = jnp.zeros((BOTH, 1), jnp.float32)
    new_out = jnp.zeros((BOTH, HD), jnp.float32)
    for j in range(STEPS):
        w = jnp.exp2(new_scores[j] - new_top)
        new_total += w
        new_out += w.astype(jnp.bfloat16).astype(jnp.float32) * nv[j : j + 1, :]

    lane = lax.broadcasted_iota(jnp.int32, (BOTH, HD), 1)
    half_lane = lane[:ROWS]
    token = lax.broadcasted_iota(jnp.int32, (BOTH, block_width), 1)
    owner = jnp.full((requests, HD), -1, jnp.int32)
    slot_lane = lax.broadcasted_iota(jnp.int32, (requests, HD), 1)
    for s in range(slots):
        owner = jnp.where(slot_lane == s, sreq_in[s], owner)
    hot = (lax.broadcasted_iota(jnp.int32, (requests, HD), 0) == owner).astype(jnp.float32)
    hot_slots = hot[:, :slots].astype(jnp.bfloat16)
    hot_twice = jnp.concatenate([hot_slots, hot_slots], axis=1)
    row_owner = owner[:BOTH]

    loads[0].wait()

    def turn_keys(it, carry):
        for u in range(TURNS):
            k_turned[it * TURNS + u] = k_vm[it * TURNS + u].T
        return carry

    lax.fori_loop(0, slots // TURNS, turn_keys, 0)
    loads[1].wait()

    for dz in LINE_Z[::-1]:
        block = peer_at(NZ - dz, 0)
        wait_bytes(q_all.at[block], line_sem.at[dz])
        for dx in LINE_X:
            send_query(block, peer_at(0, dx), query_sem.at[1])
    handed = NZ * len(LINE_X)
    wait_bytes(q_all.at[pl.ds(0, handed)], query_sem.at[1])

    def score_slots(it, top):
        for u in range(UNROLL):
            s = it * UNROLL + u
            r = sreq_in[s]
            live = jnp.clip(len_in[r] - sblk_in[s] * block_width, 0, block_width)
            sc = jnp.dot(q_all[r], k_turned[s], preferred_element_type=jnp.float32)
            sc = jnp.where(token < live, sc * scale, masked_score)
            scores[s] = sc
            top = jnp.where(lane == s, jnp.max(sc, axis=1, keepdims=True), top)
        return top

    top = lax.fori_loop(
        0, slots // UNROLL, score_slots, jnp.full((BOTH, HD), masked_score, jnp.float32)
    )

    request_top = jnp.full((BOTH, HD), masked_score, jnp.float32)
    for r in range(requests):
        m = jnp.max(jnp.where(row_owner == r, top, masked_score), axis=1, keepdims=True)
        request_top = jnp.where(lane == r, m, request_top)
        tops[r] = jnp.broadcast_to(jnp.maximum(m, floor_score), (BOTH, HD))

    def attend(half):
        rows = slice(half * ROWS, (half + 1) * ROWS)

        def weigh_slots(it, total):
            for u in range(UNROLL):
                s = it * UNROLL + u
                m = tops[sreq_in[s], rows, :]
                w = jnp.exp2(scores[s, rows, :] - jnp.concatenate([m] * (block_width // HD), axis=1))
                total = jnp.where(half_lane == s, jnp.sum(w, axis=1, keepdims=True), total)
                out = jnp.dot(w.astype(jnp.bfloat16), v_vm[s], preferred_element_type=jnp.float32)
                outs[pl.ds(pl.multiple_of(s * ROWS, ROWS), ROWS), :] = out
            return total

        total = lax.fori_loop(
            0, slots // UNROLL, weigh_slots, jnp.zeros((ROWS, HD), jnp.float32)
        )

        request_total = lax.dot_general(
            total,
            hot,
            (((1,), (1,)), ((), ())),
            precision=lax.Precision.HIGHEST,
            preferred_element_type=jnp.float32,
        )
        request_total = jnp.concatenate(
            [request_total, jnp.zeros((ROWS, HD - requests), jnp.float32)], axis=1
        )
        pair = jnp.concatenate(
            [request_top[rows], request_total, jnp.zeros((HD - 2 * ROWS, HD), jnp.float32)], axis=0
        )
        stats[half] = pair.T[:requests].reshape(requests, 1, HD)
        for j in range(ROWS):
            o = outs[pl.ds(j, slots, stride=ROWS), :]
            high = o.astype(jnp.bfloat16)
            low = (o - high.astype(jnp.float32)).astype(jnp.bfloat16)
            table_f32[pl.ds(j, requests, stride=ROWS), :] = jnp.dot(
                hot_twice, jnp.concatenate([high, low], axis=0), preferred_element_type=jnp.float32
            )
        table[half] = table_f32[...].astype(jnp.bfloat16).reshape(requests, ROWS, HD)

        to_group(lambda peer: stats.at[half, peer], got_stats.at[half, g], 0, half)
        to_group(lambda peer: table.at[half, peer], got.at[half, g], 1, half)
        got[half, g] = table[half, g]
        got_stats[half, g] = stats[half, g]

    for half in range(HALVES):
        attend(half)

    for half in range(HALVES):
        rows = slice(half * ROWS, (half + 1) * ROWS)
        own_top = new_top[rows]
        wait_bytes(got_stats.at[half, others], recv_sem.at[0, half])
        stat_rows = got_stats[half].reshape(requests, HD)
        turned = jnp.concatenate([stat_rows, jnp.zeros((HD - requests, HD), jnp.float32)], axis=0).T
        held_top = jnp.where(half_lane < requests, turned[:ROWS], masked_score)
        held_total = turned[ROWS : 2 * ROWS]
        best = jnp.maximum(jnp.max(held_top, axis=1, keepdims=True), own_top)
        held_scale = jnp.exp2(held_top - best)
        new_scale = jnp.exp2(own_top - best)
        denominator = new_scale * new_total[rows] + jnp.sum(
            held_scale * held_total, axis=1, keepdims=True
        )
        inverse = 1.0 / denominator
        held_scale = held_scale * inverse
        attention = new_scale * inverse * new_out[rows]
        wait_bytes(got.at[half, others], recv_sem.at[1, half])
        for h in range(requests):
            attention += held_scale[:, h : h + 1] * got[half, h].astype(jnp.float32)
        att_all[half, g] = attention.astype(jnp.bfloat16)
        mine = att_all.at[half, g]
        to_group(lambda peer: mine, mine, 2, half)

    loads[2].wait()
    y = jnp.zeros((requests * STEPS, w_vm.shape[1]), jnp.float32)
    for half in range(HALVES):
        wait_bytes(att_all.at[half, others], recv_sem.at[2, half])
        att_f32[...] = att_all[half].reshape(requests * ROWS, HD).astype(jnp.float32)
        att = jnp.concatenate(
            [
                att_f32[pl.ds(h, requests * STEPS, stride=HEADS), :].astype(jnp.bfloat16)
                for h in range(HEADS)
            ],
            axis=1,
        )
        rows = pl.ds(half * HEADS * HD, HEADS * HD)
        y += jnp.dot(att, w_vm[rows, :], preferred_element_type=jnp.float32)
    y_f32[...] = y.reshape(y_f32.shape)

    for peer in pool_peers:
        pltpu.make_async_remote_copy(
            src_ref=y_f32.at[peer],
            dst_ref=y_got.at[p],
            send_sem=pool_sem.at[0],
            recv_sem=pool_sem.at[1],
            device_id={"pool": peer},
            device_id_type=MESH,
        ).start()
    wait_bytes(y_got.at[pl.ds(0, pools - 1)], pool_sem.at[1])
    result = y_f32[p]
    for peer in pool_peers:
        result += y_got[peer]
    o_ref[...] = result.astype(o_ref.dtype)

    for half in range(HALVES):
        wait_bytes(got_stats.at[half, others], send_sem.at[0, half])
        wait_bytes(got.at[half, others], send_sem.at[1, half])
        wait_bytes(att_all.at[half, others], send_sem.at[2, half])
    wait_bytes(q_all.at[others], query_sem.at[0])
    wait_bytes(y_got.at[pl.ds(0, pools - 1)], pool_sem.at[0])


def body(
    queries,
    new_keys,
    new_values,
    key_cache,
    value_cache,
    lengths,
    slot_request,
    slot_block,
    out_weight,
):
    slots, block_width, _ = key_cache.shape
    requests = lengths.shape[0]
    columns = out_weight.shape[1]
    pools = lax.axis_size("pool")
    out_rows = requests * STEPS // pools
    vmem = pl.BlockSpec(memory_space=pltpu.VMEM)
    hbm = pl.BlockSpec(memory_space=pltpu.HBM)
    pin = lambda a: pltpu.with_memory_space_constraint(a, pltpu.HBM)
    return pl.pallas_call(
        kernel,
        out_shape=jax.ShapeDtypeStruct((out_rows, columns), jnp.bfloat16),
        in_specs=[hbm] * 9,
        out_specs=vmem,
        scratch_shapes=[
            pltpu.VMEM(key_cache.shape, jnp.bfloat16),
            pltpu.VMEM((slots, HD, block_width), jnp.bfloat16),
            pltpu.VMEM(value_cache.shape, jnp.bfloat16),
            pltpu.VMEM(out_weight.shape, jnp.bfloat16),
            pltpu.VMEM((BOTH, HD), jnp.float32),
            pltpu.VMEM((requests, BOTH, HD), jnp.bfloat16),
            pltpu.VMEM((slots, BOTH, block_width), jnp.float32),
            pltpu.VMEM((requests, BOTH, HD), jnp.float32),
            pltpu.VMEM((slots * ROWS, HD), jnp.float32),
            pltpu.VMEM((requests * ROWS, HD), jnp.float32),
            pltpu.VMEM((HALVES, requests, ROWS, HD), jnp.bfloat16),
            pltpu.VMEM((HALVES, requests, 1, HD), jnp.float32),
            pltpu.VMEM((HALVES, requests, ROWS, HD), jnp.bfloat16),
            pltpu.VMEM((HALVES, requests, 1, HD), jnp.float32),
            pltpu.VMEM((HALVES, requests, ROWS, HD), jnp.bfloat16),
            pltpu.VMEM((requests * ROWS, HD), jnp.float32),
            pltpu.VMEM((pools, out_rows, columns), jnp.float32),
            pltpu.VMEM((pools, out_rows, columns), jnp.float32),
            pltpu.VMEM(queries.shape, jnp.bfloat16),
            pltpu.VMEM(new_keys.shape, jnp.bfloat16),
            pltpu.VMEM(new_values.shape, jnp.bfloat16),
            pltpu.SMEM(lengths.shape, jnp.int32),
            pltpu.SMEM(slot_request.shape, jnp.int32),
            pltpu.SMEM(slot_block.shape, jnp.int32),
            pltpu.SemaphoreType.DMA((9,)),
            pltpu.SemaphoreType.DMA((3, HALVES)),
            pltpu.SemaphoreType.DMA((3, HALVES)),
            pltpu.SemaphoreType.DMA((2,)),
            pltpu.SemaphoreType.DMA((NZ,)),
            pltpu.SemaphoreType.DMA((2,)),
        ],
        compiler_params=pltpu.CompilerParams(
            collective_id=0, has_side_effects=True, vmem_limit_bytes=48 << 20
        ),
        name="paged_attention",
    )(
        pin(queries),
        pin(new_keys),
        pin(new_values),
        pin(lengths),
        pin(slot_request),
        pin(slot_block),
        pin(key_cache),
        pin(value_cache),
        pin(out_weight),
    )


def solution(mesh):
    in_specs = (
        P("group", None, "pool"),
        P("group", None, "pool"),
        P("group", None, "pool"),
        P("group", None, "pool"),
        P("group", None, "pool"),
        P(),
        P("group"),
        P("group"),
        P("pool", "group"),
    )
    out_specs = P("pool", "group")
    return jax.shard_map(body, mesh=mesh, in_specs=in_specs, out_specs=out_specs, check_vma=False)
```

```python
import functools
import math

import jax
import jax.numpy as jnp
from jax import lax
from jax.experimental import pallas as pl
from jax.experimental.pallas import tpu as pltpu
from jax.sharding import PartitionSpec as P

HD = 128
STEPS = 4
GQA = 8
HALVES = 2
HEADS = GQA // HALVES
ROWS = STEPS * HEADS
BOTH = HALVES * ROWS
UNROLL = 32
TURNS = 4
NX = 4
NZ = 8

EVERY = [(dz, dx) for dz in (4, 3, 5, 2, 6, 1, 7, 0) for dx in (2, 1, 3, 0) if (dz, dx) != (0, 0)]
LINE_Z = (4, 3, 5, 2, 6, 1, 7)
LINE_X = (2, 1, 3)
ROWS_NEAR = EVERY[::-1]
ROW_ORDER = (0, 1, 7, 2, 6, 3, 5, 4)

MESH = pl.DeviceIdType.MESH
masked_score = -1e30
floor_score = -1e29
log2e = math.log2(math.e)


def wait_bytes(ref, sem):
    pltpu.make_async_copy(ref, ref, sem).wait()


def kernel(
    q_hbm,
    nk_hbm,
    nv_hbm,
    len_hbm,
    sreq_hbm,
    sblk_hbm,
    k_hbm,
    v_hbm,
    w_hbm,
    o_ref,
    k_vm,
    k_turned,
    v_vm,
    w_vm,
    q_f32,
    q_all,
    scores,
    tops,
    outs,
    table_f32,
    table,
    stats,
    got,
    got_stats,
    att_all,
    att_f32,
    y_f32,
    y_got,
    q_in,
    nk_in,
    nv_in,
    len_in,
    sreq_in,
    sblk_in,
    load_sem,
    send_sem,
    recv_sem,
    pool_sem,
    line_sem,
    query_sem,
    row_sem,
):
    slots, block_width = k_vm.shape[0], k_vm.shape[1]
    requests = q_all.shape[0]
    pools = y_got.shape[0]
    g = lax.axis_index("group")
    p = lax.axis_index("pool")
    z, x = g // NX, g % NX
    scale = log2e / math.sqrt(HD)

    loads = [
        pltpu.make_async_copy(k_hbm, k_vm, load_sem.at[0]),
        pltpu.make_async_copy(v_hbm, v_vm, load_sem.at[1]),
        pltpu.make_async_copy(w_hbm, w_vm, load_sem.at[2]),
        pltpu.make_async_copy(q_hbm, q_in, load_sem.at[3]),
        pltpu.make_async_copy(nk_hbm, nk_in, load_sem.at[4]),
        pltpu.make_async_copy(nv_hbm, nv_in, load_sem.at[5]),
        pltpu.make_async_copy(len_hbm, len_in, load_sem.at[6]),
        pltpu.make_async_copy(sreq_hbm, sreq_in, load_sem.at[7]),
        pltpu.make_async_copy(sblk_hbm, sblk_in, load_sem.at[8]),
    ]
    for load in loads[3:] + loads[:3]:
        load.start()

    def peer_at(dz, dx):
        return lax.rem(z + dz, NZ) * NX + lax.rem(x + dx, NX)

    peers = [peer_at(dz, dx) for dz, dx in EVERY]
    others = pl.ds(0, len(peers))
    pool_peers = [lax.rem(p + d, pools) for d in (4, 5, 3, 2, 6, 7, 1)]

    barrier = pltpu.get_barrier_semaphore()
    for peer in [peer_at(dz, 0) for dz in LINE_Z] + [peer_at(0, dx) for dx in LINE_X]:
        pl.semaphore_signal(barrier, inc=1, device_id={"group": peer}, device_id_type=MESH)
    for peer in pool_peers:
        pl.semaphore_signal(barrier, inc=1, device_id={"pool": peer}, device_id_type=MESH)

    loads[3].wait()
    q_rows = q_in[0].astype(jnp.float32)
    for half in range(HALVES):
        for h in range(HEADS):
            at = (half * HEADS + h) * HD
            q_f32[pl.ds(half * ROWS + h, STEPS, stride=HEADS), :] = q_rows[:, at : at + HD]
    own_q = q_f32[...]
    q_all[g] = own_q.astype(jnp.bfloat16)

    pl.semaphore_wait(barrier, len(LINE_Z) + len(LINE_X) + len(pool_peers))

    def send(src, dst, peer, phase, half):
        pltpu.make_async_remote_copy(
            src_ref=src,
            dst_ref=dst,
            send_sem=send_sem.at[phase, half],
            recv_sem=recv_sem.at[phase, half],
            device_id={"group": peer},
            device_id_type=MESH,
        ).start()

    def send_query(owner, target, sem):
        pltpu.make_async_remote_copy(
            src_ref=q_all.at[owner],
            dst_ref=q_all.at[owner],
            send_sem=query_sem.at[0],
            recv_sem=sem,
            device_id={"group": target},
            device_id_type=MESH,
        ).start()

    for dz in LINE_Z:
        send_query(g, peer_at(dz, 0), line_sem.at[dz])
    for dx in LINE_X:
        send_query(g, peer_at(0, dx), query_sem.at[1])

    for load in loads[4:]:
        load.wait()
    row_step = lax.broadcasted_iota(jnp.int32, (BOTH, 1), 0) % ROWS // HEADS
    nk = nk_in[0].astype(jnp.float32)
    nv = nv_in[0].astype(jnp.float32)
    new_scores = []
    for j in range(STEPS):
        s = jnp.sum(own_q * nk[j : j + 1, :], axis=1, keepdims=True) * scale
        new_scores.append(jnp.where(row_step >= j, s, masked_score))
    new_top = functools.reduce(jnp.maximum, new_scores)
    new_total = jnp.zeros((BOTH, 1), jnp.float32)
    new_out = jnp.zeros((BOTH, HD), jnp.float32)
    for j in range(STEPS):
        w = jnp.exp2(new_scores[j] - new_top)
        new_total += w
        new_out += w.astype(jnp.bfloat16).astype(jnp.float32) * nv[j : j + 1, :]

    lane = lax.broadcasted_iota(jnp.int32, (BOTH, HD), 1)
    half_lane = lane[:ROWS]
    token = lax.broadcasted_iota(jnp.int32, (BOTH, block_width), 1)
    owner = jnp.full((requests, HD), -1, jnp.int32)
    slot_lane = lax.broadcasted_iota(jnp.int32, (requests, HD), 1)
    for s in range(slots):
        owner = jnp.where(slot_lane == s, sreq_in[s], owner)
    hot = (lax.broadcasted_iota(jnp.int32, (requests, HD), 0) == owner).astype(jnp.float32)
    hot_slots = hot[:, :slots].astype(jnp.bfloat16)
    hot_twice = jnp.concatenate([hot_slots, hot_slots], axis=1)
    row_owner = owner[:BOTH]

    loads[0].wait()

    def turn_keys(it, carry):
        for u in range(TURNS):
            k_turned[it * TURNS + u] = k_vm[it * TURNS + u].T
        return carry

    lax.fori_loop(0, slots // TURNS, turn_keys, 0)
    loads[1].wait()

    for dz in LINE_Z[::-1]:
        block = peer_at(NZ - dz, 0)
        wait_bytes(q_all.at[block], line_sem.at[dz])
        for dx in LINE_X:
            send_query(block, peer_at(0, dx), query_sem.at[1])
    handed = NZ * len(LINE_X)
    wait_bytes(q_all.at[pl.ds(0, handed)], query_sem.at[1])

    def score_slots(it, top):
        for u in range(UNROLL):
            s = it * UNROLL + u
            r = sreq_in[s]
            live = jnp.clip(len_in[r] - sblk_in[s] * block_width, 0, block_width)
            sc = jnp.dot(q_all[r], k_turned[s], preferred_element_type=jnp.float32)
            sc = jnp.where(token < live, sc * scale, masked_score)
            scores[s] = sc
            top = jnp.where(lane == s, jnp.max(sc, axis=1, keepdims=True), top)
        return top

    top = lax.fori_loop(
        0, slots // UNROLL, score_slots, jnp.full((BOTH, HD), masked_score, jnp.float32)
    )

    request_top = jnp.full((BOTH, HD), masked_score, jnp.float32)
    for r in range(requests):
        m = jnp.max(jnp.where(row_owner == r, top, masked_score), axis=1, keepdims=True)
        request_top = jnp.where(lane == r, m, request_top)
        tops[r] = jnp.broadcast_to(jnp.maximum(m, floor_score), (BOTH, HD))

    def attend(half):
        rows = slice(half * ROWS, (half + 1) * ROWS)

        def weigh_slots(it, total):
            for u in range(UNROLL):
                s = it * UNROLL + u
                m = tops[sreq_in[s], rows, :]
                w = jnp.exp2(scores[s, rows, :] - jnp.concatenate([m] * (block_width // HD), axis=1))
                total = jnp.where(half_lane == s, jnp.sum(w, axis=1, keepdims=True), total)
                out = jnp.dot(w.astype(jnp.bfloat16), v_vm[s], preferred_element_type=jnp.float32)
                outs[pl.ds(pl.multiple_of(s * ROWS, ROWS), ROWS), :] = out
            return total

        total = lax.fori_loop(
            0, slots // UNROLL, weigh_slots, jnp.zeros((ROWS, HD), jnp.float32)
        )

        request_total = lax.dot_general(
            total,
            hot,
            (((1,), (1,)), ((), ())),
            precision=lax.Precision.HIGHEST,
            preferred_element_type=jnp.float32,
        )
        request_total = jnp.concatenate(
            [request_total, jnp.zeros((ROWS, HD - requests), jnp.float32)], axis=1
        )
        pair = jnp.concatenate(
            [request_top[rows], request_total, jnp.zeros((HD - 2 * ROWS, HD), jnp.float32)], axis=0
        )
        stats[half] = pair.T[:requests].reshape(requests, 1, HD)
        for j in range(ROWS):
            o = outs[pl.ds(j, slots, stride=ROWS), :]
            high = o.astype(jnp.bfloat16)
            low = (o - high.astype(jnp.float32)).astype(jnp.bfloat16)
            table_f32[pl.ds(j, requests, stride=ROWS), :] = jnp.dot(
                hot_twice, jnp.concatenate([high, low], axis=0), preferred_element_type=jnp.float32
            )
        table[half] = table_f32[...].astype(jnp.bfloat16).reshape(requests, ROWS, HD)

        for peer in peers:
            send(stats.at[half, peer], got_stats.at[half, g], peer, 0, half)
            send(table.at[half, peer], got.at[half, g], peer, 1, half)
        got[half, g] = table[half, g]
        got_stats[half, g] = stats[half, g]

    for half in range(HALVES):
        attend(half)

    for half in range(HALVES):
        rows = slice(half * ROWS, (half + 1) * ROWS)
        own_top = new_top[rows]
        wait_bytes(got_stats.at[half, others], recv_sem.at[0, half])
        stat_rows = got_stats[half].reshape(requests, HD)
        turned = jnp.concatenate([stat_rows, jnp.zeros((HD - requests, HD), jnp.float32)], axis=0).T
        held_top = jnp.where(half_lane < requests, turned[:ROWS], masked_score)
        held_total = turned[ROWS : 2 * ROWS]
        best = jnp.maximum(jnp.max(held_top, axis=1, keepdims=True), own_top)
        held_scale = jnp.exp2(held_top - best)
        new_scale = jnp.exp2(own_top - best)
        denominator = new_scale * new_total[rows] + jnp.sum(
            held_scale * held_total, axis=1, keepdims=True
        )
        inverse = 1.0 / denominator
        held_scale = held_scale * inverse
        attention = new_scale * inverse * new_out[rows]
        wait_bytes(got.at[half, others], recv_sem.at[1, half])
        for h in range(requests):
            attention += held_scale[:, h : h + 1] * got[half, h].astype(jnp.float32)
        att_all[half, g] = attention.astype(jnp.bfloat16)
        mine = att_all.at[half, g]
        for dz, dx in ROWS_NEAR:
            pltpu.make_async_remote_copy(
                src_ref=mine,
                dst_ref=mine,
                send_sem=send_sem.at[2, half],
                recv_sem=row_sem.at[half, dz],
                device_id={"group": peer_at(dz, dx)},
                device_id_type=MESH,
            ).start()

    loads[2].wait()
    for dz in ROW_ORDER:
        block = lax.rem(z + NZ - dz, NZ)
        arriving = NX if dz else NX - 1
        members = pl.ds(pl.multiple_of(block * NX, NX), NX)
        heads = []
        for half in range(HALVES):
            wait_bytes(att_all.at[half, pl.ds(0, arriving)], row_sem.at[half, dz])
            att_f32[half] = att_all[half, members].reshape(NX * ROWS, HD).astype(jnp.float32)
            for h in range(HEADS):
                head = att_f32[half, pl.ds(h, NX * STEPS, stride=HEADS), :]
                heads.append(head.astype(jnp.bfloat16))
        y_f32[block] = jnp.dot(
            jnp.concatenate(heads, axis=1), w_vm[...], preferred_element_type=jnp.float32
        )

        @pl.when(block != p)
        def _():
            pltpu.make_async_remote_copy(
                src_ref=y_f32.at[block],
                dst_ref=y_got.at[p],
                send_sem=pool_sem.at[0],
                recv_sem=pool_sem.at[1],
                device_id={"pool": block},
                device_id_type=MESH,
            ).start()

    wait_bytes(y_got.at[pl.ds(0, pools - 1)], pool_sem.at[1])
    result = y_f32[p]
    for peer in pool_peers:
        result += y_got[peer]
    o_ref[...] = result.astype(o_ref.dtype)

    for half in range(HALVES):
        wait_bytes(got_stats.at[half, others], send_sem.at[0, half])
        wait_bytes(got.at[half, others], send_sem.at[1, half])
        wait_bytes(att_all.at[half, others], send_sem.at[2, half])
    wait_bytes(q_all.at[others], query_sem.at[0])
    wait_bytes(y_got.at[pl.ds(0, pools - 1)], pool_sem.at[0])


def body(
    queries,
    new_keys,
    new_values,
    key_cache,
    value_cache,
    lengths,
    slot_request,
    slot_block,
    out_weight,
):
    slots, block_width, _ = key_cache.shape
    requests = lengths.shape[0]
    columns = out_weight.shape[1]
    pools = lax.axis_size("pool")
    out_rows = requests * STEPS // pools
    vmem = pl.BlockSpec(memory_space=pltpu.VMEM)
    hbm = pl.BlockSpec(memory_space=pltpu.HBM)
    pin = lambda a: pltpu.with_memory_space_constraint(a, pltpu.HBM)
    return pl.pallas_call(
        kernel,
        out_shape=jax.ShapeDtypeStruct((out_rows, columns), jnp.bfloat16),
        in_specs=[hbm] * 9,
        out_specs=vmem,
        scratch_shapes=[
            pltpu.VMEM(key_cache.shape, jnp.bfloat16),
            pltpu.VMEM((slots, HD, block_width), jnp.bfloat16),
            pltpu.VMEM(value_cache.shape, jnp.bfloat16),
            pltpu.VMEM(out_weight.shape, jnp.bfloat16),
            pltpu.VMEM((BOTH, HD), jnp.float32),
            pltpu.VMEM((requests, BOTH, HD), jnp.bfloat16),
            pltpu.VMEM((slots, BOTH, block_width), jnp.float32),
            pltpu.VMEM((requests, BOTH, HD), jnp.float32),
            pltpu.VMEM((slots * ROWS, HD), jnp.float32),
            pltpu.VMEM((requests * ROWS, HD), jnp.float32),
            pltpu.VMEM((HALVES, requests, ROWS, HD), jnp.bfloat16),
            pltpu.VMEM((HALVES, requests, 1, HD), jnp.float32),
            pltpu.VMEM((HALVES, requests, ROWS, HD), jnp.bfloat16),
            pltpu.VMEM((HALVES, requests, 1, HD), jnp.float32),
            pltpu.VMEM((HALVES, requests, ROWS, HD), jnp.bfloat16),
            pltpu.VMEM((HALVES, NX * ROWS, HD), jnp.float32),
            pltpu.VMEM((pools, out_rows, columns), jnp.float32),
            pltpu.VMEM((pools, out_rows, columns), jnp.float32),
            pltpu.VMEM(queries.shape, jnp.bfloat16),
            pltpu.VMEM(new_keys.shape, jnp.bfloat16),
            pltpu.VMEM(new_values.shape, jnp.bfloat16),
            pltpu.SMEM(lengths.shape, jnp.int32),
            pltpu.SMEM(slot_request.shape, jnp.int32),
            pltpu.SMEM(slot_block.shape, jnp.int32),
            pltpu.SemaphoreType.DMA((9,)),
            pltpu.SemaphoreType.DMA((3, HALVES)),
            pltpu.SemaphoreType.DMA((3, HALVES)),
            pltpu.SemaphoreType.DMA((2,)),
            pltpu.SemaphoreType.DMA((NZ,)),
            pltpu.SemaphoreType.DMA((2,)),
            pltpu.SemaphoreType.DMA((HALVES, NZ)),
        ],
        compiler_params=pltpu.CompilerParams(
            collective_id=0, has_side_effects=True, vmem_limit_bytes=48 << 20
        ),
        name="paged_attention",
    )(
        pin(queries),
        pin(new_keys),
        pin(new_values),
        pin(lengths),
        pin(slot_request),
        pin(slot_block),
        pin(key_cache),
        pin(value_cache),
        pin(out_weight),
    )


def solution(mesh):
    in_specs = (
        P("group", None, "pool"),
        P("group", None, "pool"),
        P("group", None, "pool"),
        P("group", None, "pool"),
        P("group", None, "pool"),
        P(),
        P("group"),
        P("group"),
        P("pool", "group"),
    )
    out_specs = P("pool", "group")
    return jax.shard_map(body, mesh=mesh, in_specs=in_specs, out_specs=out_specs, check_vma=False)
```

```python
import functools
import math

import jax
import jax.numpy as jnp
from jax import lax
from jax.experimental import pallas as pl
from jax.experimental.pallas import tpu as pltpu
from jax.sharding import PartitionSpec as P

HD = 128
STEPS = 4
GQA = 8
HALVES = 2
HEADS = GQA // HALVES
ROWS = STEPS * HEADS
BOTH = HALVES * ROWS
UNROLL = 32
TURNS = 4
NX = 4
NZ = 8

EVERY = [(dz, dx) for dz in (4, 3, 5, 2, 6, 1, 7, 0) for dx in (2, 1, 3, 0) if (dz, dx) != (0, 0)]
LINE_Z = (4, 3, 5, 2, 6, 1, 7)
LINE_X = (2, 1, 3)
ROWS_NEAR = EVERY[::-1]
ROW_ORDER = (0, 7, 1, 6, 2, 5, 3, 4)

MESH = pl.DeviceIdType.MESH
masked_score = -1e30
floor_score = -1e29
log2e = math.log2(math.e)


def wait_bytes(ref, sem):
    pltpu.make_async_copy(ref, ref, sem).wait()


def kernel(
    q_hbm,
    nk_hbm,
    nv_hbm,
    len_hbm,
    sreq_hbm,
    sblk_hbm,
    k_hbm,
    v_hbm,
    w_hbm,
    o_ref,
    k_vm,
    k_turned,
    v_vm,
    w_vm,
    q_f32,
    q_all,
    scores,
    tops,
    outs,
    table_f32,
    table,
    stats,
    got,
    got_stats,
    att_all,
    att_f32,
    y_f32,
    y_got,
    q_in,
    nk_in,
    nv_in,
    len_in,
    sreq_in,
    sblk_in,
    load_sem,
    send_sem,
    recv_sem,
    pool_sem,
    line_sem,
    query_sem,
    row_sem,
):
    slots, block_width = k_vm.shape[0], k_vm.shape[1]
    requests = q_all.shape[0]
    pools = y_got.shape[0]
    g = lax.axis_index("group")
    p = lax.axis_index("pool")
    z, x = g // NX, g % NX
    scale = log2e / math.sqrt(HD)

    loads = [
        pltpu.make_async_copy(k_hbm, k_vm, load_sem.at[0]),
        pltpu.make_async_copy(v_hbm, v_vm, load_sem.at[1]),
        pltpu.make_async_copy(w_hbm, w_vm, load_sem.at[2]),
        pltpu.make_async_copy(q_hbm, q_in, load_sem.at[3]),
        pltpu.make_async_copy(nk_hbm, nk_in, load_sem.at[4]),
        pltpu.make_async_copy(nv_hbm, nv_in, load_sem.at[5]),
        pltpu.make_async_copy(len_hbm, len_in, load_sem.at[6]),
        pltpu.make_async_copy(sreq_hbm, sreq_in, load_sem.at[7]),
        pltpu.make_async_copy(sblk_hbm, sblk_in, load_sem.at[8]),
    ]
    for load in loads[3:] + loads[:3]:
        load.start()

    def peer_at(dz, dx):
        return lax.rem(z + dz, NZ) * NX + lax.rem(x + dx, NX)

    peers = [peer_at(dz, dx) for dz, dx in EVERY]
    others = pl.ds(0, len(peers))
    pool_peers = [lax.rem(p + d, pools) for d in (4, 5, 3, 2, 6, 7, 1)]

    barrier = pltpu.get_barrier_semaphore()
    for peer in [peer_at(dz, 0) for dz in LINE_Z] + [peer_at(0, dx) for dx in LINE_X]:
        pl.semaphore_signal(barrier, inc=1, device_id={"group": peer}, device_id_type=MESH)
    for peer in pool_peers:
        pl.semaphore_signal(barrier, inc=1, device_id={"pool": peer}, device_id_type=MESH)

    loads[3].wait()
    q_rows = q_in[0].astype(jnp.float32)
    for half in range(HALVES):
        for h in range(HEADS):
            at = (half * HEADS + h) * HD
            q_f32[pl.ds(half * ROWS + h, STEPS, stride=HEADS), :] = q_rows[:, at : at + HD]
    own_q = q_f32[...]
    q_all[g] = own_q.astype(jnp.bfloat16)

    pl.semaphore_wait(barrier, len(LINE_Z) + len(LINE_X) + len(pool_peers))

    def send(src, dst, peer, phase, half):
        pltpu.make_async_remote_copy(
            src_ref=src,
            dst_ref=dst,
            send_sem=send_sem.at[phase, half],
            recv_sem=recv_sem.at[phase, half],
            device_id={"group": peer},
            device_id_type=MESH,
        ).start()

    def send_query(owner, target, sem):
        pltpu.make_async_remote_copy(
            src_ref=q_all.at[owner],
            dst_ref=q_all.at[owner],
            send_sem=query_sem.at[0],
            recv_sem=sem,
            device_id={"group": target},
            device_id_type=MESH,
        ).start()

    for dz in LINE_Z:
        send_query(g, peer_at(dz, 0), line_sem.at[dz])
    for dx in LINE_X:
        send_query(g, peer_at(0, dx), query_sem.at[1])

    for load in loads[4:]:
        load.wait()
    row_step = lax.broadcasted_iota(jnp.int32, (BOTH, 1), 0) % ROWS // HEADS
    nk = nk_in[0].astype(jnp.float32)
    nv = nv_in[0].astype(jnp.float32)
    new_scores = []
    for j in range(STEPS):
        s = jnp.sum(own_q * nk[j : j + 1, :], axis=1, keepdims=True) * scale
        new_scores.append(jnp.where(row_step >= j, s, masked_score))
    new_top = functools.reduce(jnp.maximum, new_scores)
    new_total = jnp.zeros((BOTH, 1), jnp.float32)
    new_out = jnp.zeros((BOTH, HD), jnp.float32)
    for j in range(STEPS):
        w = jnp.exp2(new_scores[j] - new_top)
        new_total += w
        new_out += w.astype(jnp.bfloat16).astype(jnp.float32) * nv[j : j + 1, :]

    lane = lax.broadcasted_iota(jnp.int32, (BOTH, HD), 1)
    half_lane = lane[:ROWS]
    token = lax.broadcasted_iota(jnp.int32, (BOTH, block_width), 1)
    owner = jnp.full((requests, HD), -1, jnp.int32)
    slot_lane = lax.broadcasted_iota(jnp.int32, (requests, HD), 1)
    for s in range(slots):
        owner = jnp.where(slot_lane == s, sreq_in[s], owner)
    hot = (lax.broadcasted_iota(jnp.int32, (requests, HD), 0) == owner).astype(jnp.float32)
    hot_slots = hot[:, :slots].astype(jnp.bfloat16)
    hot_twice = jnp.concatenate([hot_slots, hot_slots], axis=1)
    row_owner = owner[:BOTH]

    loads[0].wait()

    def turn_keys(it, carry):
        for u in range(TURNS):
            k_turned[it * TURNS + u] = k_vm[it * TURNS + u].T
        return carry

    lax.fori_loop(0, slots // TURNS, turn_keys, 0)
    loads[1].wait()

    for dz in LINE_Z[::-1]:
        block = peer_at(NZ - dz, 0)
        wait_bytes(q_all.at[block], line_sem.at[dz])
        for dx in LINE_X:
            send_query(block, peer_at(0, dx), query_sem.at[1])
    handed = NZ * len(LINE_X)
    wait_bytes(q_all.at[pl.ds(0, handed)], query_sem.at[1])

    def score_slots(it, top):
        for u in range(UNROLL):
            s = it * UNROLL + u
            r = sreq_in[s]
            live = jnp.clip(len_in[r] - sblk_in[s] * block_width, 0, block_width)
            sc = jnp.dot(q_all[r], k_turned[s], preferred_element_type=jnp.float32)
            sc = jnp.where(token < live, sc * scale, masked_score)
            scores[s] = sc
            top = jnp.where(lane == s, jnp.max(sc, axis=1, keepdims=True), top)
        return top

    top = lax.fori_loop(
        0, slots // UNROLL, score_slots, jnp.full((BOTH, HD), masked_score, jnp.float32)
    )

    request_top = jnp.full((BOTH, HD), masked_score, jnp.float32)
    for r in range(requests):
        m = jnp.max(jnp.where(row_owner == r, top, masked_score), axis=1, keepdims=True)
        request_top = jnp.where(lane == r, m, request_top)
        tops[r] = jnp.broadcast_to(jnp.maximum(m, floor_score), (BOTH, HD))

    def attend(half):
        rows = slice(half * ROWS, (half + 1) * ROWS)

        def weigh_slots(it, total):
            for u in range(UNROLL):
                s = it * UNROLL + u
                m = tops[sreq_in[s], rows, :]
                w = jnp.exp2(scores[s, rows, :] - jnp.concatenate([m] * (block_width // HD), axis=1))
                total = jnp.where(half_lane == s, jnp.sum(w, axis=1, keepdims=True), total)
                out = jnp.dot(w.astype(jnp.bfloat16), v_vm[s], preferred_element_type=jnp.float32)
                outs[pl.ds(pl.multiple_of(s * ROWS, ROWS), ROWS), :] = out
            return total

        total = lax.fori_loop(
            0, slots // UNROLL, weigh_slots, jnp.zeros((ROWS, HD), jnp.float32)
        )

        request_total = lax.dot_general(
            total,
            hot,
            (((1,), (1,)), ((), ())),
            precision=lax.Precision.HIGHEST,
            preferred_element_type=jnp.float32,
        )
        request_total = jnp.concatenate(
            [request_total, jnp.zeros((ROWS, HD - requests), jnp.float32)], axis=1
        )
        pair = jnp.concatenate(
            [request_top[rows], request_total, jnp.zeros((HD - 2 * ROWS, HD), jnp.float32)], axis=0
        )
        stats[half] = pair.T[:requests].reshape(requests, 1, HD)
        for j in range(ROWS):
            o = outs[pl.ds(j, slots, stride=ROWS), :]
            high = o.astype(jnp.bfloat16)
            low = (o - high.astype(jnp.float32)).astype(jnp.bfloat16)
            table_f32[pl.ds(j, requests, stride=ROWS), :] = jnp.dot(
                hot_twice, jnp.concatenate([high, low], axis=0), preferred_element_type=jnp.float32
            )
        table[half] = table_f32[...].astype(jnp.bfloat16).reshape(requests, ROWS, HD)

        for peer in peers:
            send(stats.at[half, peer], got_stats.at[half, g], peer, 0, half)
            send(table.at[half, peer], got.at[half, g], peer, 1, half)
        got[half, g] = table[half, g]
        got_stats[half, g] = stats[half, g]

    for half in range(HALVES):
        attend(half)

    for half in range(HALVES):
        rows = slice(half * ROWS, (half + 1) * ROWS)
        own_top = new_top[rows]
        wait_bytes(got_stats.at[half, others], recv_sem.at[0, half])
        stat_rows = got_stats[half].reshape(requests, HD)
        turned = jnp.concatenate([stat_rows, jnp.zeros((HD - requests, HD), jnp.float32)], axis=0).T
        held_top = jnp.where(half_lane < requests, turned[:ROWS], masked_score)
        held_total = turned[ROWS : 2 * ROWS]
        best = jnp.maximum(jnp.max(held_top, axis=1, keepdims=True), own_top)
        held_scale = jnp.exp2(held_top - best)
        new_scale = jnp.exp2(own_top - best)
        denominator = new_scale * new_total[rows] + jnp.sum(
            held_scale * held_total, axis=1, keepdims=True
        )
        inverse = 1.0 / denominator
        held_scale = held_scale * inverse
        attention = new_scale * inverse * new_out[rows]
        wait_bytes(got.at[half, others], recv_sem.at[1, half])
        for h in range(requests):
            attention += held_scale[:, h : h + 1] * got[half, h].astype(jnp.float32)
        att_all[half, g] = attention.astype(jnp.bfloat16)
        mine = att_all.at[half, g]
        for dz, dx in ROWS_NEAR:
            pltpu.make_async_remote_copy(
                src_ref=mine,
                dst_ref=mine,
                send_sem=send_sem.at[2, half],
                recv_sem=row_sem.at[half, dz],
                device_id={"group": peer_at(dz, dx)},
                device_id_type=MESH,
            ).start()

    loads[2].wait()
    for dz in ROW_ORDER:
        block = lax.rem(z + NZ - dz, NZ)
        arriving = NX if dz else NX - 1
        members = pl.ds(pl.multiple_of(block * NX, NX), NX)
        heads = []
        for half in range(HALVES):
            wait_bytes(att_all.at[half, pl.ds(0, arriving)], row_sem.at[half, dz])
            att_f32[half] = att_all[half, members].reshape(NX * ROWS, HD).astype(jnp.float32)
            for h in range(HEADS):
                head = att_f32[half, pl.ds(h, NX * STEPS, stride=HEADS), :]
                heads.append(head.astype(jnp.bfloat16))
        y_f32[block] = jnp.dot(
            jnp.concatenate(heads, axis=1), w_vm[...], preferred_element_type=jnp.float32
        )

        @pl.when(block != p)
        def _():
            pltpu.make_async_remote_copy(
                src_ref=y_f32.at[block],
                dst_ref=y_got.at[p],
                send_sem=pool_sem.at[0],
                recv_sem=pool_sem.at[1],
                device_id={"pool": block},
                device_id_type=MESH,
            ).start()

    wait_bytes(y_got.at[pl.ds(0, pools - 1)], pool_sem.at[1])
    result = y_f32[p]
    for peer in pool_peers:
        result += y_got[peer]
    o_ref[...] = result.astype(o_ref.dtype)

    for half in range(HALVES):
        wait_bytes(got_stats.at[half, others], send_sem.at[0, half])
        wait_bytes(got.at[half, others], send_sem.at[1, half])
        wait_bytes(att_all.at[half, others], send_sem.at[2, half])
    wait_bytes(q_all.at[others], query_sem.at[0])
    wait_bytes(y_got.at[pl.ds(0, pools - 1)], pool_sem.at[0])


def body(
    queries,
    new_keys,
    new_values,
    key_cache,
    value_cache,
    lengths,
    slot_request,
    slot_block,
    out_weight,
):
    slots, block_width, _ = key_cache.shape
    requests = lengths.shape[0]
    columns = out_weight.shape[1]
    pools = lax.axis_size("pool")
    out_rows = requests * STEPS // pools
    vmem = pl.BlockSpec(memory_space=pltpu.VMEM)
    hbm = pl.BlockSpec(memory_space=pltpu.HBM)
    pin = lambda a: pltpu.with_memory_space_constraint(a, pltpu.HBM)
    return pl.pallas_call(
        kernel,
        out_shape=jax.ShapeDtypeStruct((out_rows, columns), jnp.bfloat16),
        in_specs=[hbm] * 9,
        out_specs=vmem,
        scratch_shapes=[
            pltpu.VMEM(key_cache.shape, jnp.bfloat16),
            pltpu.VMEM((slots, HD, block_width), jnp.bfloat16),
            pltpu.VMEM(value_cache.shape, jnp.bfloat16),
            pltpu.VMEM(out_weight.shape, jnp.bfloat16),
            pltpu.VMEM((BOTH, HD), jnp.float32),
            pltpu.VMEM((requests, BOTH, HD), jnp.bfloat16),
            pltpu.VMEM((slots, BOTH, block_width), jnp.float32),
            pltpu.VMEM((requests, BOTH, HD), jnp.float32),
            pltpu.VMEM((slots * ROWS, HD), jnp.float32),
            pltpu.VMEM((requests * ROWS, HD), jnp.float32),
            pltpu.VMEM((HALVES, requests, ROWS, HD), jnp.bfloat16),
            pltpu.VMEM((HALVES, requests, 1, HD), jnp.float32),
            pltpu.VMEM((HALVES, requests, ROWS, HD), jnp.bfloat16),
            pltpu.VMEM((HALVES, requests, 1, HD), jnp.float32),
            pltpu.VMEM((HALVES, requests, ROWS, HD), jnp.bfloat16),
            pltpu.VMEM((HALVES, NX * ROWS, HD), jnp.float32),
            pltpu.VMEM((pools, out_rows, columns), jnp.float32),
            pltpu.VMEM((pools, out_rows, columns), jnp.float32),
            pltpu.VMEM(queries.shape, jnp.bfloat16),
            pltpu.VMEM(new_keys.shape, jnp.bfloat16),
            pltpu.VMEM(new_values.shape, jnp.bfloat16),
            pltpu.SMEM(lengths.shape, jnp.int32),
            pltpu.SMEM(slot_request.shape, jnp.int32),
            pltpu.SMEM(slot_block.shape, jnp.int32),
            pltpu.SemaphoreType.DMA((9,)),
            pltpu.SemaphoreType.DMA((3, HALVES)),
            pltpu.SemaphoreType.DMA((3, HALVES)),
            pltpu.SemaphoreType.DMA((2,)),
            pltpu.SemaphoreType.DMA((NZ,)),
            pltpu.SemaphoreType.DMA((2,)),
            pltpu.SemaphoreType.DMA((HALVES, NZ)),
        ],
        compiler_params=pltpu.CompilerParams(
            collective_id=0, has_side_effects=True, vmem_limit_bytes=48 << 20
        ),
        name="paged_attention",
    )(
        pin(queries),
        pin(new_keys),
        pin(new_values),
        pin(lengths),
        pin(slot_request),
        pin(slot_block),
        pin(key_cache),
        pin(value_cache),
        pin(out_weight),
    )


def solution(mesh):
    in_specs = (
        P("group", None, "pool"),
        P("group", None, "pool"),
        P("group", None, "pool"),
        P("group", None, "pool"),
        P("group", None, "pool"),
        P(),
        P("group"),
        P("group"),
        P("pool", "group"),
    )
    out_specs = P("pool", "group")
    return jax.shard_map(body, mesh=mesh, in_specs=in_specs, out_specs=out_specs, check_vma=False)
```
